32 devices in a mesh: dp: 16 (over z, y, core), tensor: 2 (over x).
Axes of the slice: x: 2, y: 2, z: 4, core: 2. Of those that a mesh axis runs over, the one named last changes fastest.
Arguments:
- acts: bfloat16 [16384, 8192], P('dp', 'tensor'), may hold values from -6 to 6
- out_grads: bfloat16 [16384, 28672], P('dp', 'tensor'), may hold values from -6 to 6
- proj_in: bfloat16 [64, 8192], P(None, 'tensor'), may hold values from -0.0625 to 0.0625
- proj_out: bfloat16 [64, 28672], P(None, 'tensor'), may hold values from -0.03125 to 0.03125
- lengths: int32 [64], P('dp'), may hold values from 1 to 256, 8192 in all
- queries: float32 [512, 4096], P('tensor', 'dp'), may hold values from -6 to 6
- query_ids: int32 [512], P('tensor'), may hold values from 0 to 63
Outputs:
- scores: float32 [64, 512], P('dp', 'tensor')
The draws below stay inside these ranges and needn't reach their ends.
All inputs are finite; a program needn't handle non-finite values. No bound on the sum of `lengths` on one device may be relied on, other than what follows from the above.
Results may differ from the reference program's by a relative error of at most 0.0003.
Values sent between devices are 32-bit elements; how exact they have to be, the bound alone decides.
No kernel may reach another device: no remote copies, remote signals or barrier semaphores. Data moves between devices by JAX's collectives and lax.ppermute only.
A program may use at most 128 MiB of HBM per device.

```python
import math
import jax
import jax.numpy as jnp
import numpy as np
from jax import lax

D = 8192
FF = 28672
RANK_IN = 64
RANK_OUT = 64
QUERIES = 512
SLOT = 256
EXAMPLES = 64
TOKENS = 16384


def set_ends(result, stream_key, least, largest):
    longest = result.shape.index(max(result.shape))
    spots = []
    for shift in (0, 1):
        where = [jax.random.randint(jax.random.fold_in(stream_key, axis), (), 0, length) for axis, length in enumerate(result.shape)]
        where[longest] = (where[longest] + shift) % result.shape[longest]
        spots.append(tuple(where))
    return result.at[spots[0]].set(least).at[spots[1]].set(largest)


def shard_levels(own_key, shape, pieces, least, largest):
    factor_of, own = 1.0, jax.random.fold_in(own_key, 6)
    for dim, blocks in pieces:
        steps = jnp.exp(jax.random.uniform(jax.random.fold_in(own, dim), (blocks,), jnp.float32, least / len(pieces), largest / len(pieces)))
        factor_of = factor_of * jnp.repeat(steps, shape[dim] // blocks).reshape([-1 if axis == dim else 1 for axis in range(len(shape))])
    return factor_of


def length_profile(count, total, reach, slope):
    loads = [(1 << 20) // math.isqrt(grade ** slope) + 1 for grade in range(2, count + 1)]
    surplus, counts = total - reach - (count - 1), [1] * (count - 1)
    while surplus > 0:
        movable = [i for i in range(count - 1) if counts[i] < reach]
        pool, remaining = sum([loads[i] for i in movable]), surplus
        for i in movable:
            addition = min(reach - counts[i], max(1, remaining * loads[i] // pool), surplus)
            counts[i] = counts[i] + addition
            surplus = surplus - addition
    return np.array([reach] + counts)


def uneven_parts(key, count, total, limit, skew):
    if count == 2:
        one = jax.random.randint(key, (), max(1, total - limit), min(limit, total - 1) + 1)
        return jnp.stack([one, total - one])
    sizes = jnp.asarray(length_profile(count, total, limit, skew), jnp.int32)
    couples = (count - 1) // 2
    donor, receiver = sizes[1:1 + 2 * couples:2], sizes[2:2 + 2 * couples:2]
    room = jnp.minimum(donor - 1, limit - receiver)
    moved = jax.random.randint(jax.random.fold_in(key, 1), (couples,), 0, 1 << 20) % (room + 1)
    sizes = sizes.at[1:1 + 2 * couples:2].set(donor - moved).at[2:2 + 2 * couples:2].set(receiver + moved)
    return sizes[jax.random.permutation(jax.random.fold_in(key, 2), count)]


def centred(rng, dims, scale, reach, cuts=(), kind=jnp.bfloat16):
    array = scale * jax.random.normal(rng, dims, jnp.float32)
    if cuts:
        array = array * shard_levels(rng, dims, cuts, -0.22, 0.18)
    return jnp.clip(array, -reach, reach).astype(kind)


def setup_inputs(seed: int = 0) -> dict:
    splits = jax.random.split(jax.random.key(seed), 8)
    return {
        "acts": centred(splits[0], (TOKENS, D), 1.0, 6.0, ((0, 16), (1, 2))),
        "out_grads": centred(splits[1], (TOKENS, FF), 1.0, 6.0, ((0, 16), (1, 2))),
        "proj_in": centred(splits[2], (RANK_IN, D), D ** -0.5, 0.0625, ((1, 2),)),
        "proj_out": centred(splits[3], (RANK_OUT, FF), FF ** -0.5, 0.03125, ((1, 2),)),
        "lengths": uneven_parts(splits[4], EXAMPLES, EXAMPLES * SLOT // 2, SLOT, 0).astype(jnp.int32),
        "queries": centred(splits[5], (QUERIES, RANK_IN * RANK_OUT), 1.0, 6.0, ((0, 2), (1, 16)), jnp.float32),
        "query_ids": set_ends(jax.random.randint(splits[6], (QUERIES,), 0, EXAMPLES), jax.random.fold_in(splits[6], 1), 0, EXAMPLES - 1).astype(jnp.int32),
    }


def reference(acts, out_grads, proj_in, proj_out, lengths, queries, query_ids):

    def one_example(items):
        act_rows, grad_rows, used = items
        proj_acts = jnp.dot(act_rows, proj_in.T, preferred_element_type=jnp.float32)
        proj_grads = jnp.dot(grad_rows, proj_out.T, preferred_element_type=jnp.float32)
        valid = (jnp.arange(SLOT, dtype=jnp.int32) < used).astype(jnp.float32)
        masked = proj_grads * valid[:, None]
        return jnp.dot(masked.T, proj_acts, precision=lax.Precision.HIGHEST).reshape(-1)
    kron = lax.map(one_example, (acts.reshape(EXAMPLES, SLOT, D), out_grads.reshape(EXAMPLES, SLOT, FF), lengths))
    unit = kron / jnp.sqrt(lax.optimization_barrier(jnp.sum(kron * kron, axis=1, keepdims=True)) + 1e-06)
    scores = jnp.dot(unit, queries.T, precision=lax.Precision.HIGHEST)
    same = jnp.arange(EXAMPLES, dtype=jnp.int32)[:, None] == query_ids[None, :]
    return jnp.where(same, jnp.zeros_like(scores), scores)
```

```python
import functools

import jax
import jax.numpy as jnp
from jax import lax
from jax.experimental import pallas as pl
from jax.experimental.pallas import tpu as pltpu
from jax.sharding import PartitionSpec as P

BLOCK = 64
NEAR = 8
NT = (((1,), (1,)), ((), ()))
TN = (((0,), (0,)), ((), ()))
ANY = pl.BlockSpec(memory_space=pl.ANY)
VMEM = pl.BlockSpec(memory_space=pltpu.VMEM)


def xor_pairs(size, mask):
    return [(i, i ^ mask) for i in range(size)]


def swap(x, mask):
    return lax.ppermute(x, "dp", xor_pairs(lax.axis_size("dp"), mask))


def project_kernel(peer, count, slot, lengths, acts, grads, proj_in, proj_out, out,
                   used, act_buf, grad_buf, in_buf, out_buf, sems, small):
    per = slot // BLOCK
    blocks = count * per
    first = 0
    if peer is not None:
        mine = lax.axis_index("tensor")
        first = (1 - mine if peer else mine) * count
    rank = proj_out.shape[0]

    def copies(j):
        row = pl.multiple_of(first * slot + j * BLOCK, BLOCK)
        return (
            pltpu.make_async_copy(grads.at[pl.ds(row, BLOCK)], grad_buf.at[j], sems.at[0, j]),
            pltpu.make_async_copy(acts.at[pl.ds(row, BLOCK)], act_buf.at[j], sems.at[1, j]),
        )

    def left(j):
        return used[first + j // per] - (j % per) * BLOCK

    get_used = pltpu.make_async_copy(lengths, used, small.at[0])
    get_out = pltpu.make_async_copy(proj_out, out_buf, small.at[1])
    get_in = pltpu.make_async_copy(proj_in, in_buf, small.at[2])
    get_used.start()
    get_out.start()
    get_in.start()
    get_used.wait()

    @pl.loop(0, blocks)
    def _(j):
        @pl.when(left(j) > 0)
        def _():
            for copy in copies(j):
                copy.start()

    get_out.wait()
    get_in.wait()

    @pl.loop(0, blocks)
    def _(j):
        rows = left(j)

        @pl.when(rows > 0)
        def _():
            for copy in copies(j):
                copy.wait()
            part_grads = lax.dot_general(
                grad_buf[j], out_buf[...], NT, preferred_element_type=jnp.float32
            )
            part_acts = lax.dot_general(
                act_buf[j], in_buf[...], NT, preferred_element_type=jnp.float32
            )
            joined = jnp.concatenate([part_grads, part_acts], axis=1)
            row = lax.broadcasted_iota(jnp.int32, joined.shape, 0)
            out[j] = jnp.where(row < rows, joined, 0.0)

        @pl.when(rows <= 0)
        def _():
            out[j] = jnp.zeros((BLOCK, 2 * rank), jnp.float32)


def project(peer, count, slot, lengths, acts, grads, proj_in, proj_out):
    blocks = count * slot // BLOCK
    width = proj_out.shape[0] + proj_in.shape[0]
    rows = blocks * BLOCK
    bytes_accessed = 2 * (rows + width // 2) * (acts.shape[1] + grads.shape[1])
    return pl.pallas_call(
        functools.partial(project_kernel, peer, count, slot),
        out_shape=jax.ShapeDtypeStruct((blocks, BLOCK, width), jnp.float32),
        in_specs=[ANY] * 5,
        out_specs=VMEM,
        scratch_shapes=[
            pltpu.SMEM(lengths.shape, jnp.int32),
            pltpu.VMEM((blocks, BLOCK, acts.shape[1]), acts.dtype),
            pltpu.VMEM((blocks, BLOCK, grads.shape[1]), grads.dtype),
            pltpu.VMEM(proj_in.shape, proj_in.dtype),
            pltpu.VMEM(proj_out.shape, proj_out.dtype),
            pltpu.SemaphoreType.DMA((2, blocks)),
            pltpu.SemaphoreType.DMA((3,)),
        ],
        compiler_params=pltpu.CompilerParams(vmem_limit_bytes=44 << 20),
        cost_estimate=pl.CostEstimate(
            flops=width * rows * (acts.shape[1] + grads.shape[1]),
            bytes_accessed=bytes_accessed,
            transcendentals=0,
        ),
        name="project",
    )(lengths, acts, grads, proj_in, proj_out)


def unit_kernel(count, slot, rank, *refs):
    parts, outs, square, cols = refs[:-3], refs[-3], refs[-2], refs[-1]
    near = outs.shape[2]
    group = lax.axis_index("dp") // near
    split, per = cols.shape[1], square.shape[0] // cols.shape[1]
    for e in range(count):
        total = parts[0][e]
        for part in parts[1:]:
            total = total + part[e]
        kron = lax.dot_general(
            total[:, :rank], total[:, rank:], TN,
            precision=lax.Precision.HIGHEST, preferred_element_type=jnp.float32,
        )
        norm = jnp.sqrt(jnp.sum(kron * kron, keepdims=True) + 1e-06)
        square[...] = kron / norm
        cols[e] = jnp.concatenate(
            [square[pl.ds(c, split, stride=per), :] for c in range(per)], axis=1
        )
        for r in range(outs.shape[0]):
            start = pl.multiple_of((group ^ r) * near, near)
            outs[r, e] = cols[e, pl.ds(start, near), :]


def units(parts, count, slot, rank, split):
    width = parts[0].shape[-1]
    rest = width - rank
    near = min(NEAR, split)
    parts = [part.reshape(count, slot, width) for part in parts]
    return pl.pallas_call(
        functools.partial(unit_kernel, count, slot, rank),
        out_shape=jax.ShapeDtypeStruct(
            (split // near, count, near, rank * rest // split), jnp.float32
        ),
        in_specs=[VMEM] * len(parts),
        out_specs=VMEM,
        scratch_shapes=[
            pltpu.VMEM((rank, rest), jnp.float32),
            pltpu.VMEM((count, split, rank * rest // split), jnp.float32),
        ],
        name="units",
    )(*parts)


def hi_lo(x):
    hi = x.astype(jnp.bfloat16)
    return hi, (x - hi.astype(jnp.float32)).astype(jnp.bfloat16)


def score_kernel(sources, *refs):
    rows_of, blocks, out = refs[:sources], refs[sources:-1], refs[-1]
    low = lax.axis_index("dp") % len(blocks)
    count = rows_of[0].shape[0]
    total = jnp.zeros(out.shape, jnp.float32)
    for m, block in enumerate(blocks):
        rows = jnp.concatenate(
            [ref[e, pl.ds(low ^ m, 1), :] for ref in rows_of for e in range(count)], axis=0
        )
        rows_hi, rows_lo = hi_lo(rows)
        block_hi, block_lo = hi_lo(block[...])
        both = lax.dot_general(
            jnp.concatenate([rows_hi, rows_lo], axis=0), block_hi, NT,
            preferred_element_type=jnp.float32,
        )
        cross = lax.dot_general(rows_hi, block_lo, NT, preferred_element_type=jnp.float32)
        total = total + (both[: rows.shape[0]] + (both[rows.shape[0] :] + cross))
    out[...] = total


def partial_scores(rows_of, blocks):
    rows = sum(part.shape[0] for part in rows_of)
    return pl.pallas_call(
        functools.partial(score_kernel, len(rows_of)),
        out_shape=jax.ShapeDtypeStruct((rows, blocks[0].shape[0]), jnp.float32),
        in_specs=[VMEM] * (len(rows_of) + len(blocks)),
        out_specs=VMEM,
        name="scores",
    )(*rows_of, *blocks)


def gather_near(queries, near):
    blocks = {0: queries}
    if near == 8:
        half = queries.shape[0] // 2
        blocks[2] = swap(queries, 2)
        blocks[4] = swap(queries, 4)
        blocks[6] = jnp.concatenate(
            [swap(blocks[4][:half], 2), swap(blocks[2][half:], 4)], axis=0
        )
        for m in (0, 2, 4, 6):
            blocks[m ^ 1] = swap(blocks[m], 1)
    else:
        for m in range(1, near):
            blocks[m] = swap(queries, m)
    return [blocks[m] for m in range(near)]


def on_device(acts, out_grads, proj_in, proj_out, lengths, queries, query_ids):
    rank_out = proj_out.shape[0]
    ex_count = lengths.shape[0]
    slot = acts.shape[0] // ex_count
    split = lax.axis_size("dp")
    near = min(NEAR, split)
    tensors = lax.axis_size("tensor")
    halves = tensors == 2 and ex_count % 2 == 0
    args = (lengths, acts, out_grads, proj_in, proj_out)
    blocks = gather_near(queries, near)
    if halves:
        count = ex_count // 2
        theirs = project(True, count, slot, *args)
        arrived = lax.ppermute(theirs, "tensor", [(0, 1), (1, 0)])
        mine = project(False, count, slot, *args)
        parts = [mine, arrived]
    else:
        count = ex_count
        parts = [lax.psum(project(None, count, slot, *args), "tensor")]
    unit = units(parts, count, slot, rank_out, split)
    rows_of = []
    for r in range(split // near):
        got = unit[r]
        far = got if r == 0 else swap(got, r * near)
        rows_of.append(far)
        if halves:
            both = [(2 * i + t, 2 * (i ^ (r * near)) + 1 - t) for i in range(split) for t in (0, 1)]
            rows_of.append(lax.ppermute(got, ("dp", "tensor"), both))
    sums = partial_scores(rows_of, blocks)
    sums = sums.reshape(split // near, ex_count, -1)
    scores = sums[0]
    for r in range(1, split // near):
        scores = scores + swap(sums[r], r * near)
    if halves:
        scores = jnp.where(
            lax.axis_index("tensor") == 0, scores, jnp.roll(scores, count, axis=0)
        )
    example_ids = lax.axis_index("dp") * ex_count + lax.broadcasted_iota(
        jnp.int32, (ex_count, 1), 0
    )
    same = example_ids == query_ids[None, :]
    return jnp.where(same, jnp.zeros_like(scores), scores)


def solution(mesh):
    in_specs = (
        P("dp", "tensor"),
        P("dp", "tensor"),
        P(None, "tensor"),
        P(None, "tensor"),
        P("dp"),
        P("tensor", "dp"),
        P("tensor"),
    )
    out_specs = P("dp", "tensor")
    return jax.shard_map(
        on_device, mesh=mesh, in_specs=in_specs, out_specs=out_specs, check_vma=False
    )
```

```python
import functools

import jax
import jax.numpy as jnp
from jax import lax
from jax.experimental import pallas as pl
from jax.experimental.pallas import tpu as pltpu
from jax.sharding import PartitionSpec as P

BLOCK = 64
NEAR_BITS = 3
NT = (((1,), (1,)), ((), ()))
TN = (((0,), (0,)), ((), ()))
HBM = pl.BlockSpec(memory_space=pltpu.HBM)
VMEM = pl.BlockSpec(memory_space=pltpu.VMEM)


def xor_pairs(size, mask):
    return [(i, i ^ mask) for i in range(size)]


def swap(x, mask):
    return lax.ppermute(x, "dp", xor_pairs(lax.axis_size("dp"), mask))


def project_kernel(peer, count, slot, lengths, acts, grads, proj_in, proj_out, out,
                   used, act_buf, grad_buf, in_buf, out_buf, sems, small):
    per = slot // BLOCK
    blocks = count * per
    first = 0
    if peer is not None:
        mine = lax.axis_index("tensor")
        first = (1 - mine if peer else mine) * count
    rank = proj_out.shape[0]

    def copies(j):
        row = pl.multiple_of(first * slot + j * BLOCK, BLOCK)
        return (
            pltpu.make_async_copy(grads.at[pl.ds(row, BLOCK)], grad_buf.at[j], sems.at[0, j]),
            pltpu.make_async_copy(acts.at[pl.ds(row, BLOCK)], act_buf.at[j], sems.at[1, j]),
        )

    def left(j):
        return used[first + j // per] - (j % per) * BLOCK

    get_used = pltpu.make_async_copy(lengths, used, small.at[0])
    get_out = pltpu.make_async_copy(proj_out, out_buf, small.at[1])
    get_in = pltpu.make_async_copy(proj_in, in_buf, small.at[2])
    get_used.start()
    get_out.start()
    for copy in copies(0):
        copy.start()
    get_in.start()
    get_used.wait()

    @pl.loop(1, blocks)
    def _(j):
        @pl.when(left(j) > 0)
        def _():
            for copy in copies(j):
                copy.start()

    get_out.wait()
    get_in.wait()

    @pl.loop(0, blocks)
    def _(j):
        rows = left(j)

        @pl.when(rows > 0)
        def _():
            for copy in copies(j):
                copy.wait()
            part_grads = lax.dot_general(
                grad_buf[j], out_buf[...], NT, preferred_element_type=jnp.float32
            )
            part_acts = lax.dot_general(
                act_buf[j], in_buf[...], NT, preferred_element_type=jnp.float32
            )
            joined = jnp.concatenate([part_grads, part_acts], axis=1)
            row = lax.broadcasted_iota(jnp.int32, joined.shape, 0)
            out[j] = jnp.where(row < rows, joined, 0.0)

        @pl.when(rows <= 0)
        def _():
            out[j] = jnp.zeros((BLOCK, 2 * rank), jnp.float32)


def project(peer, count, slot, *args):
    lengths, acts, grads, proj_in, proj_out = args
    blocks = count * slot // BLOCK
    width = proj_out.shape[0] + proj_in.shape[0]
    rows = blocks * BLOCK
    depth = acts.shape[1] + grads.shape[1]
    return pl.pallas_call(
        functools.partial(project_kernel, peer, count, slot),
        out_shape=jax.ShapeDtypeStruct((blocks, BLOCK, width), jnp.float32),
        in_specs=[HBM] * 5,
        out_specs=VMEM,
        scratch_shapes=[
            pltpu.SMEM(lengths.shape, jnp.int32),
            pltpu.VMEM((blocks, BLOCK, acts.shape[1]), acts.dtype),
            pltpu.VMEM((blocks, BLOCK, grads.shape[1]), grads.dtype),
            pltpu.VMEM(proj_in.shape, proj_in.dtype),
            pltpu.VMEM(proj_out.shape, proj_out.dtype),
            pltpu.SemaphoreType.DMA((2, blocks)),
            pltpu.SemaphoreType.DMA((3,)),
        ],
        compiler_params=pltpu.CompilerParams(
            vmem_limit_bytes=2 * (rows + width) * depth + (6 << 20)
        ),
        cost_estimate=pl.CostEstimate(
            flops=width * rows * depth, bytes_accessed=2 * rows * depth, transcendentals=0
        ),
        name="project",
    )(*[pltpu.with_memory_space_constraint(x, pltpu.HBM) for x in args])


def hi_lo(x):
    hi = x.astype(jnp.bfloat16)
    return hi, (x - hi.astype(jnp.float32)).astype(jnp.bfloat16)


def unit_kernel(count, rank, near, rest, *refs):
    parts, outs, square, cols = refs[: -2 - len(rest)], refs[-2 - len(rest) : -2], refs[-2], refs[-1]
    here = lax.axis_index("dp")
    split, per = cols.shape[1], square.shape[1] // cols.shape[1]
    for e in range(count):
        total = parts[0][e]
        for part in parts[1:]:
            total = total + part[e]
        grads = jnp.concatenate(hi_lo(total[:, :rank]), axis=1)
        acts = jnp.concatenate(hi_lo(total[:, rank:]), axis=1)
        both = lax.dot_general(grads, acts, TN, preferred_element_type=jnp.float32)
        width = total.shape[1] - rank
        kron = (both[:rank, :width] + both[rank:, width:]) + (
            both[:rank, width:] + both[rank:, :width]
        )
        norm = jnp.sqrt(jnp.sum(kron * kron, keepdims=True) + 1e-06)
        square[e] = kron / norm
        cols[e] = jnp.concatenate(
            [square[e, pl.ds(c, split, stride=per), :] for c in range(per)], axis=1
        )
        for r, out in zip(rest, outs):
            for k, m in enumerate(near):
                out[e, k : k + 1] = cols[e, pl.ds(here ^ (r ^ m), 1), :]


def units(parts, count, slot, rank, split, near, rest):
    width = parts[0].shape[-1]
    piece = rank * (width - rank) // split
    parts = [part.reshape(count, slot, width) for part in parts]
    return pl.pallas_call(
        functools.partial(unit_kernel, count, rank, near, rest),
        out_shape=[jax.ShapeDtypeStruct((count, len(near), piece), jnp.float32) for _ in rest],
        in_specs=[VMEM] * len(parts),
        out_specs=[VMEM] * len(rest),
        scratch_shapes=[
            pltpu.VMEM((count, rank, width - rank), jnp.float32),
            pltpu.VMEM((count, split, piece), jnp.float32),
        ],
        compiler_params=pltpu.CompilerParams(vmem_limit_bytes=8 << 20),
        name="units",
    )(*parts)


def score_kernel(sources, groups, *refs):
    rows_of, blocks, outs = refs[:sources], refs[sources:-groups], refs[-groups:]
    count = rows_of[0].shape[0]
    rows_all = count * sources
    total = jnp.zeros((rows_all, outs[0].shape[1]), jnp.float32)
    for m, block in enumerate(blocks):
        rows = jnp.concatenate(
            [ref[e, m : m + 1, :] for ref in rows_of for e in range(count)], axis=0
        )
        rows_hi, rows_lo = hi_lo(rows)
        block_hi, block_lo = hi_lo(block[...])
        both = lax.dot_general(
            jnp.concatenate([rows_hi, rows_lo], axis=0), block_hi, NT,
            preferred_element_type=jnp.float32,
        )
        cross = lax.dot_general(rows_hi, block_lo, NT, preferred_element_type=jnp.float32)
        total = total + (both[:rows_all] + (both[rows_all:] + cross))
    each = rows_all // len(outs)
    swapped = lax.axis_index("tensor") == 1
    for g, out in enumerate(outs):
        mine = total[g * each : (g + 1) * each]
        if each > count:
            turned = jnp.concatenate([mine[count:], mine[:count]], axis=0)
            mine = jnp.where(swapped, turned, mine)
        out[...] = mine


def partial_scores(rows_of, blocks, groups):
    each = sum(part.shape[0] for part in rows_of) // groups
    return pl.pallas_call(
        functools.partial(score_kernel, len(rows_of), groups),
        out_shape=[jax.ShapeDtypeStruct((each, blocks[0].shape[0]), jnp.float32)] * groups,
        in_specs=[VMEM] * (len(rows_of) + len(blocks)),
        out_specs=[VMEM] * groups,
        compiler_params=pltpu.CompilerParams(vmem_limit_bytes=16 << 20),
        name="scores",
    )(*rows_of, *blocks)


def span(bits):
    masks = [0]
    for bit in bits:
        masks = masks + [m ^ bit for m in masks]
    return masks


def on_device(acts, out_grads, proj_in, proj_out, lengths, queries, query_ids):
    rank_out = proj_out.shape[0]
    ex_count = lengths.shape[0]
    slot = acts.shape[0] // ex_count
    split = lax.axis_size("dp")
    bits = [1 << i for i in range(split.bit_length() - 1)]
    near = span(bits[:NEAR_BITS])
    rest = span(bits[NEAR_BITS:])
    halves = lax.axis_size("tensor") == 2 and ex_count % 2 == 0
    args = (lengths, acts, out_grads, proj_in, proj_out)
    if halves:
        count = ex_count // 2
        theirs = project(True, count, slot, *args)
        theirs, queries = lax.optimization_barrier((theirs, queries))
        arrived = lax.ppermute(theirs, "tensor", [(0, 1), (1, 0)])
        parts = [project(False, count, slot, *args), arrived]
    else:
        count = ex_count
        parts = [lax.psum(project(None, count, slot, *args), "tensor")]
    blocks = {0: queries}
    for m in near:
        if m == 1 or m % 2 == 0 and m > 0:
            blocks[m] = swap(queries, m)
    own = units(parts, count, slot, rank_out, split, near, rest)
    rows_of = []
    for r, got in zip(rest, own):
        rows_of.append(got if r == 0 else swap(got, r))
        if halves:
            both = [(2 * i + t, 2 * (i ^ r) + 1 - t) for i in range(split) for t in (0, 1)]
            rows_of.append(lax.ppermute(got, ("dp", "tensor"), both))
    rows_of[1], blocks = lax.optimization_barrier((rows_of[1], blocks))
    for m in near:
        if m > 1 and m % 2 == 1:
            blocks[m] = swap(blocks[m ^ 1], 1)
    sums = partial_scores(rows_of, [blocks[m] for m in near], len(rest))
    scores = sums[0]
    for r, got in zip(rest[1:], sums[1:]):
        scores = scores + swap(got, r)
    example_ids = lax.axis_index("dp") * ex_count + lax.broadcasted_iota(
        jnp.int32, (ex_count, 1), 0
    )
    same = example_ids == query_ids[None, :]
    return jnp.where(same, jnp.zeros_like(scores), scores)


def solution(mesh):
    in_specs = (
        P("dp", "tensor"),
        P("dp", "tensor"),
        P(None, "tensor"),
        P(None, "tensor"),
        P("dp"),
        P("tensor", "dp"),
        P("tensor"),
    )
    out_specs = P("dp", "tensor")
    return jax.shard_map(
        on_device, mesh=mesh, in_specs=in_specs, out_specs=out_specs, check_vma=False
    )
```

```python
import functools

import jax
import jax.numpy as jnp
from jax import lax
from jax.experimental import pallas as pl
from jax.experimental.pallas import tpu as pltpu
from jax.sharding import PartitionSpec as P

BLOCK = 64
NEAR_BITS = 3
NT = (((1,), (1,)), ((), ()))
TN = (((0,), (0,)), ((), ()))
HBM = pl.BlockSpec(memory_space=pltpu.HBM)
VMEM = pl.BlockSpec(memory_space=pltpu.VMEM)


def xor_pairs(size, mask):
    return [(i, i ^ mask) for i in range(size)]


def swap(x, mask):
    return lax.ppermute(x, "dp", xor_pairs(lax.axis_size("dp"), mask))


def project_kernel(peer, count, slot, lengths, acts, grads, proj_in, proj_out, out,
                   used, act_buf, grad_buf, in_buf, out_buf, sems, small):
    per = slot // BLOCK
    blocks = count * per
    first = 0
    if peer is not None:
        mine = lax.axis_index("tensor")
        first = (1 - mine if peer else mine) * count
    rank = proj_out.shape[0]

    def copies(j):
        row = pl.multiple_of(first * slot + j * BLOCK, BLOCK)
        return (
            pltpu.make_async_copy(grads.at[pl.ds(row, BLOCK)], grad_buf.at[j], sems.at[0, j]),
            pltpu.make_async_copy(acts.at[pl.ds(row, BLOCK)], act_buf.at[j], sems.at[1, j]),
        )

    def left(j):
        return used[first + j // per] - (j % per) * BLOCK

    get_used = pltpu.make_async_copy(lengths, used, small.at[0])
    get_out = pltpu.make_async_copy(proj_out, out_buf, small.at[1])
    get_in = pltpu.make_async_copy(proj_in, in_buf, small.at[2])
    get_used.start()
    get_out.start()
    for copy in copies(0):
        copy.start()
    get_in.start()
    get_used.wait()

    @pl.loop(1, blocks)
    def _(j):
        @pl.when(left(j) > 0)
        def _():
            for copy in copies(j):
                copy.start()

    get_out.wait()
    get_in.wait()

    @pl.loop(0, blocks)
    def _(j):
        rows = left(j)

        @pl.when(rows > 0)
        def _():
            for copy in copies(j):
                copy.wait()
            part_grads = lax.dot_general(
                grad_buf[j], out_buf[...], NT, preferred_element_type=jnp.float32
            )
            part_acts = lax.dot_general(
                act_buf[j], in_buf[...], NT, preferred_element_type=jnp.float32
            )
            joined = jnp.concatenate([part_grads, part_acts], axis=1)
            row = lax.broadcasted_iota(jnp.int32, joined.shape, 0)
            out[j] = jnp.where(row < rows, joined, 0.0)

        @pl.when(rows <= 0)
        def _():
            out[j] = jnp.zeros((BLOCK, 2 * rank), jnp.float32)


def project(peer, count, slot, *args):
    lengths, acts, grads, proj_in, proj_out = args
    blocks = count * slot // BLOCK
    width = proj_out.shape[0] + proj_in.shape[0]
    rows = blocks * BLOCK
    depth = acts.shape[1] + grads.shape[1]
    return pl.pallas_call(
        functools.partial(project_kernel, peer, count, slot),
        out_shape=jax.ShapeDtypeStruct((blocks, BLOCK, width), jnp.float32),
        in_specs=[HBM] * 5,
        out_specs=VMEM,
        scratch_shapes=[
            pltpu.SMEM(lengths.shape, jnp.int32),
            pltpu.VMEM((blocks, BLOCK, acts.shape[1]), acts.dtype),
            pltpu.VMEM((blocks, BLOCK, grads.shape[1]), grads.dtype),
            pltpu.VMEM(proj_in.shape, proj_in.dtype),
            pltpu.VMEM(proj_out.shape, proj_out.dtype),
            pltpu.SemaphoreType.DMA((2, blocks)),
            pltpu.SemaphoreType.DMA((3,)),
        ],
        compiler_params=pltpu.CompilerParams(
            vmem_limit_bytes=2 * (rows + width) * depth + (6 << 20)
        ),
        cost_estimate=pl.CostEstimate(
            flops=width * rows * depth, bytes_accessed=2 * rows * depth, transcendentals=0
        ),
        name="project",
    )(*[pltpu.with_memory_space_constraint(x, pltpu.HBM) for x in args])


def hi_lo(x):
    hi = x.astype(jnp.bfloat16)
    return hi, (x - hi.astype(jnp.float32)).astype(jnp.bfloat16)


def unit_kernel(count, rank, near, rest, *refs):
    parts, out, square, cols = refs[:-3], refs[-3], refs[-2], refs[-1]
    here = lax.axis_index("dp")
    split, per = cols.shape[1], square.shape[1] // cols.shape[1]
    for e in range(count):
        total = parts[0][e]
        for part in parts[1:]:
            total = total + part[e]
        grads = jnp.concatenate(hi_lo(total[:, :rank]), axis=1)
        acts = jnp.concatenate(hi_lo(total[:, rank:]), axis=1)
        both = lax.dot_general(grads, acts, TN, preferred_element_type=jnp.float32)
        width = total.shape[1] - rank
        kron = (both[:rank, :width] + both[rank:, width:]) + (
            both[:rank, width:] + both[rank:, :width]
        )
        norm = jnp.sqrt(jnp.sum(kron * kron, keepdims=True) + 1e-06)
        square[e] = kron / norm
        cols[e] = jnp.concatenate(
            [square[e, pl.ds(c, split, stride=per), :] for c in range(per)], axis=1
        )
        for g, r in enumerate(rest):
            for k, m in enumerate(near):
                out[g, e, k : k + 1] = cols[e, pl.ds(here ^ (r ^ m), 1), :]


def units(parts, count, slot, rank, split, near, rest):
    width = parts[0].shape[-1]
    piece = rank * (width - rank) // split
    parts = [part.reshape(count, slot, width) for part in parts]
    return pl.pallas_call(
        functools.partial(unit_kernel, count, rank, near, rest),
        out_shape=jax.ShapeDtypeStruct((len(rest), count, len(near), piece), jnp.float32),
        in_specs=[VMEM] * len(parts),
        out_specs=VMEM,
        scratch_shapes=[
            pltpu.VMEM((count, rank, width - rank), jnp.float32),
            pltpu.VMEM((count, split, piece), jnp.float32),
        ],
        compiler_params=pltpu.CompilerParams(vmem_limit_bytes=8 << 20),
        name="units",
    )(*parts)


def score_kernel(sources, halves, *refs):
    rows_of, blocks, outs = refs[:sources], refs[sources:-sources], refs[-sources:]
    count = rows_of[0].shape[0]
    rows_all = count * sources
    total = jnp.zeros((rows_all, outs[0].shape[1]), jnp.float32)
    for m, block in enumerate(blocks):
        rows = jnp.concatenate(
            [ref[e, m : m + 1, :] for ref in rows_of for e in range(count)], axis=0
        )
        rows_hi, rows_lo = hi_lo(rows)
        block_hi, block_lo = hi_lo(block[...])
        both = lax.dot_general(
            jnp.concatenate([rows_hi, rows_lo], axis=0), block_hi, NT,
            preferred_element_type=jnp.float32,
        )
        cross = lax.dot_general(rows_hi, block_lo, NT, preferred_element_type=jnp.float32)
        total = total + (both[:rows_all] + (both[rows_all:] + cross))
    for g, out in enumerate(outs):
        mine = total[g * count : (g + 1) * count]
        if halves:
            turned = jnp.concatenate([mine[count // 2 :], mine[: count // 2]], axis=0)
            mine = jnp.where(lax.axis_index("tensor") == 1, turned, mine)
        out[...] = mine


def partial_scores(rows_of, blocks, halves):
    sources = len(rows_of)
    shape = jax.ShapeDtypeStruct((rows_of[0].shape[0], blocks[0].shape[0]), jnp.float32)
    return pl.pallas_call(
        functools.partial(score_kernel, sources, halves),
        out_shape=[shape] * sources,
        in_specs=[VMEM] * (sources + len(blocks)),
        out_specs=[VMEM] * sources,
        compiler_params=pltpu.CompilerParams(vmem_limit_bytes=16 << 20),
        name="scores",
    )(*rows_of, *blocks)


def span(bits):
    masks = [0]
    for bit in bits:
        masks = masks + [m ^ bit for m in masks]
    return masks


def on_device(acts, out_grads, proj_in, proj_out, lengths, queries, query_ids):
    rank_out = proj_out.shape[0]
    ex_count = lengths.shape[0]
    slot = acts.shape[0] // ex_count
    split = lax.axis_size("dp")
    bits = [1 << i for i in range(split.bit_length() - 1)]
    near = span(bits[:NEAR_BITS])
    rest = span(bits[NEAR_BITS:])
    halves = lax.axis_size("tensor") == 2 and ex_count % 2 == 0
    args = (lengths, acts, out_grads, proj_in, proj_out)
    blocks = {0: queries}
    for m in near:
        if m == 1 or m % 2 == 0 and m > 0:
            blocks[m] = swap(queries, m)
    if halves:
        count = ex_count // 2
        theirs = project(True, count, slot, *args)
        arrived = lax.ppermute(theirs, "tensor", [(0, 1), (1, 0)])
        parts = [project(False, count, slot, *args), arrived]
    else:
        count = ex_count
        parts = [lax.psum(project(None, count, slot, *args), "tensor")]
    early = {m: blocks[m] for m in blocks if m < 6}
    early, parts = lax.optimization_barrier((early, parts))
    blocks = {**blocks, **early}
    own = units(parts, count, slot, rank_out, split, near, rest)
    if halves:
        own = jnp.concatenate([own, lax.ppermute(own, "tensor", [(0, 1), (1, 0)])], axis=1)
        own, blocks = lax.optimization_barrier((own, blocks))
    rows_of = [own[g] if r == 0 else swap(own[g], r) for g, r in enumerate(rest)]
    for m in near:
        if m > 1 and m % 2 == 1:
            blocks[m] = swap(blocks[m ^ 1], 1)
    sums = partial_scores(rows_of, [blocks[m] for m in near], halves)
    scores = sums[0]
    for r, got in zip(rest[1:], sums[1:]):
        scores = scores + swap(got, r)
    example_ids = lax.axis_index("dp") * ex_count + lax.broadcasted_iota(
        jnp.int32, (ex_count, 1), 0
    )
    same = example_ids == query_ids[None, :]
    return jnp.where(same, jnp.zeros_like(scores), scores)


def solution(mesh):
    in_specs = (
        P("dp", "tensor"),
        P("dp", "tensor"),
        P(None, "tensor"),
        P(None, "tensor"),
        P("dp"),
        P("tensor", "dp"),
        P("tensor"),
    )
    out_specs = P("dp", "tensor")
    return jax.shard_map(
        on_device, mesh=mesh, in_specs=in_specs, out_specs=out_specs, check_vma=False
    )
```

```python
import functools

import jax
import jax.numpy as jnp
from jax import lax
from jax.experimental import pallas as pl
from jax.experimental.pallas import tpu as pltpu
from jax.sharding import PartitionSpec as P

BLOCK = 64
NEAR_BITS = 3
NT = (((1,), (1,)), ((), ()))
TN = (((0,), (0,)), ((), ()))
HBM = pl.BlockSpec(memory_space=pltpu.HBM)
VMEM = pl.BlockSpec(memory_space=pltpu.VMEM)


def xor_pairs(size, mask):
    return [(i, i ^ mask) for i in range(size)]


def swap(x, mask):
    return lax.ppermute(x, "dp", xor_pairs(lax.axis_size("dp"), mask))


def project_kernel(peer, count, slot, held, lengths, acts, grads, *refs):
    if held:
        in_buf, out_buf, out, used, act_buf, grad_buf, sems, small = refs
    else:
        proj_in, proj_out, out, in_buf, out_buf, used, act_buf, grad_buf, sems, small = refs
    per = slot // BLOCK
    blocks = count * per
    first = 0
    if peer is not None:
        mine = lax.axis_index("tensor")
        first = (1 - mine if peer else mine) * count
    rank = out_buf.shape[0]

    def copies(j):
        row = pl.multiple_of(first * slot + j * BLOCK, BLOCK)
        return (
            pltpu.make_async_copy(grads.at[pl.ds(row, BLOCK)], grad_buf.at[j], sems.at[0, j]),
            pltpu.make_async_copy(acts.at[pl.ds(row, BLOCK)], act_buf.at[j], sems.at[1, j]),
        )

    def left(j):
        return used[first + j // per] - (j % per) * BLOCK

    get_used = pltpu.make_async_copy(lengths, used, small.at[0])
    get_used.start()
    if not held:
        get_out = pltpu.make_async_copy(proj_out, out_buf, small.at[1])
        get_in = pltpu.make_async_copy(proj_in, in_buf, small.at[2])
        get_out.start()
        get_in.start()
    for copy in copies(0):
        copy.start()
    get_used.wait()

    @pl.loop(1, blocks)
    def _(j):
        @pl.when(left(j) > 0)
        def _():
            for copy in copies(j):
                copy.start()

    if not held:
        get_out.wait()
        get_in.wait()

    @pl.loop(0, blocks)
    def _(j):
        rows = left(j)

        @pl.when(rows > 0)
        def _():
            for copy in copies(j):
                copy.wait()
            part_grads = lax.dot_general(
                grad_buf[j], out_buf[...], NT, preferred_element_type=jnp.float32
            )
            part_acts = lax.dot_general(
                act_buf[j], in_buf[...], NT, preferred_element_type=jnp.float32
            )
            joined = jnp.concatenate([part_grads, part_acts], axis=1)
            row = lax.broadcasted_iota(jnp.int32, joined.shape, 0)
            out[j] = jnp.where(row < rows, joined, 0.0)

        @pl.when(rows <= 0)
        def _():
            out[j] = jnp.zeros((BLOCK, 2 * rank), jnp.float32)


def project(peer, count, slot, *args, held=False):
    lengths, acts, grads, proj_in, proj_out = args
    blocks = count * slot // BLOCK
    width = proj_out.shape[0] + proj_in.shape[0]
    rows = blocks * BLOCK
    depth = acts.shape[1] + grads.shape[1]
    outside = 3 if held else 5
    args = [pltpu.with_memory_space_constraint(x, pltpu.HBM) for x in args[:outside]] + [
        *args[outside:]
    ]
    out_shape = [jax.ShapeDtypeStruct((blocks, BLOCK, width), jnp.float32)]
    if not held:
        out_shape += [jax.ShapeDtypeStruct(x.shape, x.dtype) for x in (proj_in, proj_out)]
    return pl.pallas_call(
        functools.partial(project_kernel, peer, count, slot, held),
        out_shape=out_shape,
        in_specs=[HBM] * outside + [VMEM] * (5 - outside),
        out_specs=[VMEM] * len(out_shape),
        scratch_shapes=[
            pltpu.SMEM(lengths.shape, jnp.int32),
            pltpu.VMEM((blocks, BLOCK, acts.shape[1]), acts.dtype),
            pltpu.VMEM((blocks, BLOCK, grads.shape[1]), grads.dtype),
            pltpu.SemaphoreType.DMA((2, blocks)),
            pltpu.SemaphoreType.DMA((3,)),
        ],
        compiler_params=pltpu.CompilerParams(vmem_limit_bytes=2 * rows * depth + (6 << 20)),
        cost_estimate=pl.CostEstimate(
            flops=width * rows * depth, bytes_accessed=2 * rows * depth, transcendentals=0
        ),
        name="project",
    )(*args)


def hi_lo(x):
    hi = x.astype(jnp.bfloat16)
    return hi, (x - hi.astype(jnp.float32)).astype(jnp.bfloat16)


def unit_kernel(count, rank, near, rest, *refs):
    parts, out, square, cols = refs[:-3], refs[-3], refs[-2], refs[-1]
    here = lax.axis_index("dp")
    split, per = cols.shape[1], square.shape[1] // cols.shape[1]
    for e in range(count):
        total = parts[0][e]
        for part in parts[1:]:
            total = total + part[e]
        grads = jnp.concatenate(hi_lo(total[:, :rank]), axis=1)
        acts = jnp.concatenate(hi_lo(total[:, rank:]), axis=1)
        both = lax.dot_general(grads, acts, TN, preferred_element_type=jnp.float32)
        width = total.shape[1] - rank
        kron = (both[:rank, :width] + both[rank:, width:]) + (
            both[:rank, width:] + both[rank:, :width]
        )
        norm = jnp.sqrt(jnp.sum(kron * kron, keepdims=True) + 1e-06)
        square[e] = kron / norm
        cols[e] = jnp.concatenate(
            [square[e, pl.ds(c, split, stride=per), :] for c in range(per)], axis=1
        )
        for g, r in enumerate(rest):
            for k, m in enumerate(near):
                out[g, e, k : k + 1] = cols[e, pl.ds(here ^ (r ^ m), 1), :]


def units(parts, count, slot, rank, split, near, rest):
    width = parts[0].shape[-1]
    piece = rank * (width - rank) // split
    parts = [part.reshape(count, slot, width) for part in parts]
    return pl.pallas_call(
        functools.partial(unit_kernel, count, rank, near, rest),
        out_shape=jax.ShapeDtypeStruct((len(rest), count, len(near), piece), jnp.float32),
        in_specs=[VMEM] * len(parts),
        out_specs=VMEM,
        scratch_shapes=[
            pltpu.VMEM((count, rank, width - rank), jnp.float32),
            pltpu.VMEM((count, split, piece), jnp.float32),
        ],
        compiler_params=pltpu.CompilerParams(vmem_limit_bytes=8 << 20),
        name="units",
    )(*parts)


def score_kernel(sources, halves, *refs):
    rows_of, blocks, outs = refs[:sources], refs[sources:-sources], refs[-sources:]
    count = rows_of[0].shape[0]
    rows_all = count * sources
    total = jnp.zeros((rows_all, outs[0].shape[1]), jnp.float32)
    for m, block in enumerate(blocks):
        rows = jnp.concatenate(
            [ref[e, m : m + 1, :] for ref in rows_of for e in range(count)], axis=0
        )
        rows_hi, rows_lo = hi_lo(rows)
        block_hi, block_lo = hi_lo(block[...])
        both = lax.dot_general(
            jnp.concatenate([rows_hi, rows_lo], axis=0), block_hi, NT,
            preferred_element_type=jnp.float32,
        )
        cross = lax.dot_general(rows_hi, block_lo, NT, preferred_element_type=jnp.float32)
        total = total + (both[:rows_all] + (both[rows_all:] + cross))
    for g, out in enumerate(outs):
        mine = total[g * count : (g + 1) * count]
        if halves:
            turned = jnp.concatenate([mine[count // 2 :], mine[: count // 2]], axis=0)
            mine = jnp.where(lax.axis_index("tensor") == 1, turned, mine)
        out[...] = mine


def partial_scores(rows_of, blocks, halves):
    sources = len(rows_of)
    shape = jax.ShapeDtypeStruct((rows_of[0].shape[0], blocks[0].shape[0]), jnp.float32)
    return pl.pallas_call(
        functools.partial(score_kernel, sources, halves),
        out_shape=[shape] * sources,
        in_specs=[VMEM] * (sources + len(blocks)),
        out_specs=[VMEM] * sources,
        compiler_params=pltpu.CompilerParams(vmem_limit_bytes=16 << 20),
        name="scores",
    )(*rows_of, *blocks)


def span(bits):
    masks = [0]
    for bit in bits:
        masks = masks + [m ^ bit for m in masks]
    return masks


def on_device(acts, out_grads, proj_in, proj_out, lengths, queries, query_ids):
    rank_out = proj_out.shape[0]
    ex_count = lengths.shape[0]
    slot = acts.shape[0] // ex_count
    split = lax.axis_size("dp")
    bits = [1 << i for i in range(split.bit_length() - 1)]
    near = span(bits[:NEAR_BITS])
    rest = span(bits[NEAR_BITS:])
    halves = lax.axis_size("tensor") == 2 and ex_count % 2 == 0
    args = (lengths, acts, out_grads, proj_in, proj_out)
    blocks = {0: queries}
    for m in near:
        if m == 1 or m % 2 == 0 and m > 0:
            blocks[m] = swap(queries, m)
    if halves:
        count = ex_count // 2
        theirs, *factors = project(True, count, slot, *args)
        arrived = lax.ppermute(theirs, "tensor", [(0, 1), (1, 0)])
        parts = [project(False, count, slot, *args[:3], *factors, held=True)[0], arrived]
    else:
        count = ex_count
        parts = [lax.psum(project(None, count, slot, *args)[0], "tensor")]
    early = [m for m in reversed(bits[:NEAR_BITS])]
    held, parts[0] = lax.optimization_barrier(([blocks[m] for m in early], parts[0]))
    blocks.update(zip(early, held))
    own = units(parts, count, slot, rank_out, split, near, rest)
    if halves:
        own = jnp.concatenate([own, lax.ppermute(own, "tensor", [(0, 1), (1, 0)])], axis=1)
        own, blocks = lax.optimization_barrier((own, blocks))
    rows_of = [own[g] if r == 0 else swap(own[g], r) for g, r in enumerate(rest)]
    for m in near:
        if m > 1 and m % 2 == 1:
            blocks[m] = swap(blocks[m ^ 1], 1)
    sums = partial_scores(rows_of, [blocks[m] for m in near], halves)
    scores = sums[0]
    for r, got in zip(rest[1:], sums[1:]):
        scores = scores + swap(got, r)
    example_ids = lax.axis_index("dp") * ex_count + lax.broadcasted_iota(
        jnp.int32, (ex_count, 1), 0
    )
    same = example_ids == query_ids[None, :]
    return jnp.where(same, jnp.zeros_like(scores), scores)


def solution(mesh):
    in_specs = (
        P("dp", "tensor"),
        P("dp", "tensor"),
        P(None, "tensor"),
        P(None, "tensor"),
        P("dp"),
        P("tensor", "dp"),
        P("tensor"),
    )
    out_specs = P("dp", "tensor")
    return jax.shard_map(
        on_device, mesh=mesh, in_specs=in_specs, out_specs=out_specs, check_vma=False
    )
```

```python
import functools

import jax
import jax.numpy as jnp
from jax import lax
from jax.experimental import pallas as pl
from jax.experimental.pallas import tpu as pltpu
from jax.sharding import PartitionSpec as P

BLOCK = 64
WINDOW = 5
NEAR_BITS = 3
NT = (((1,), (1,)), ((), ()))
TN = (((0,), (0,)), ((), ()))
HBM = pl.BlockSpec(memory_space=pltpu.HBM)
VMEM = pl.BlockSpec(memory_space=pltpu.VMEM)


def xor_pairs(size, mask):
    return [(i, i ^ mask) for i in range(size)]


def swap(x, mask):
    return lax.ppermute(x, "dp", xor_pairs(lax.axis_size("dp"), mask))


def project_kernel(peer, count, slot, held, lengths, acts, grads, *refs):
    if held:
        in_buf, out_buf, _, _, out, act_buf, grad_buf, sems, small = refs
        used = lengths
    elif peer:
        proj_in, proj_out, out, in_buf, out_buf, next_act, next_grad = refs[:7]
        used, act_buf, grad_buf, sems, small = refs[7:]
    else:
        proj_in, proj_out, out, used, in_buf, out_buf, act_buf, grad_buf, sems, small = refs
    per = slot // BLOCK
    blocks = count * per
    first = other = 0
    if peer is not None:
        mine = lax.axis_index("tensor")
        first = (1 - mine if peer else mine) * count
        other = count - first
    rank = out_buf.shape[0]

    def copies(j):
        row = pl.multiple_of(first * slot + j * BLOCK, BLOCK)
        return (
            pltpu.make_async_copy(grads.at[pl.ds(row, BLOCK)], grad_buf.at[j], sems.at[0, j]),
            pltpu.make_async_copy(acts.at[pl.ds(row, BLOCK)], act_buf.at[j], sems.at[1, j]),
        )

    def left(j):
        return used[first + j // per] - (j % per) * BLOCK

    if not held:
        get_used = pltpu.make_async_copy(lengths, used, small.at[0])
        get_used.start()
    ahead = []
    if not held:
        get_out = pltpu.make_async_copy(proj_out, out_buf, small.at[1])
        get_in = pltpu.make_async_copy(proj_in, in_buf, small.at[2])
        get_out.start()
        get_in.start()
        for copy in copies(0):
            copy.start()
    if peer:
        for e in range(count):
            row = pl.multiple_of((other + e) * slot, BLOCK)
            for data, buf in ((grads, next_grad), (acts, next_act)):
                ahead.append(
                    pltpu.make_async_copy(
                        data.at[pl.ds(row, BLOCK)], buf.at[e * per], small.at[3 + len(ahead)]
                    )
                )
    if not held:
        get_used.wait()

    def place(i):
        if not held:
            return i
        rest = i - count
        later = rest // (per - 1) * per + rest % (per - 1) + 1
        return jnp.where(i < count, i * per, later)

    def fetch(i):
        j = place(jnp.minimum(i, blocks - 1))

        @pl.when((i < blocks) & (left(j) > 0))
        def _():
            for copy in copies(j):
                copy.start()

    @pl.loop(count if held else 1, WINDOW if held else blocks)
    def _(i):
        fetch(i)

    if not held:
        get_out.wait()
        get_in.wait()

    @pl.loop(0, blocks)
    def _(i):
        j = place(i)
        rows = left(j)
        if held:
            fetch(i + WINDOW)
        if peer:

            @pl.when(i == 2)
            def _():
                for copy in ahead:
                    copy.start()

        @pl.when(rows > 0)
        def _():
            if held:

                @pl.when(i >= count)
                def _():
                    for copy in copies(j):
                        copy.wait()
            else:
                for copy in copies(j):
                    copy.wait()
            part_grads = lax.dot_general(
                grad_buf[j], out_buf[...], NT, preferred_element_type=jnp.float32
            )
            part_acts = lax.dot_general(
                act_buf[j], in_buf[...], NT, preferred_element_type=jnp.float32
            )
            joined = jnp.concatenate([part_grads, part_acts], axis=1)
            row = lax.broadcasted_iota(jnp.int32, joined.shape, 0)
            out[j] = jnp.where(row < rows, joined, 0.0)

        @pl.when(rows <= 0)
        def _():
            out[j] = jnp.zeros((BLOCK, 2 * rank), jnp.float32)

    for copy in ahead:
        copy.wait()


def project(peer, count, slot, *args, held=()):
    lengths, acts, grads = args[:3]
    blocks = count * slot // BLOCK
    factors = held[:2] if held else args[3:]
    width = factors[0].shape[0] + factors[1].shape[0]
    rows = blocks * BLOCK
    depth = acts.shape[1] + grads.shape[1]
    outside = args[:3] if held else args
    operands = [pltpu.with_memory_space_constraint(x, pltpu.HBM) for x in outside] + [*held]
    in_specs = [HBM] * len(outside) + [VMEM] * len(held)
    if held:
        operands[0], in_specs[0] = lengths, pl.BlockSpec(memory_space=pltpu.SMEM)
    bufs = [(blocks, BLOCK, acts.shape[1]), (blocks, BLOCK, grads.shape[1])]
    out_shape = [jax.ShapeDtypeStruct((blocks, BLOCK, width), jnp.float32)]
    scratch_shapes = [] if held else [pltpu.SMEM(lengths.shape, jnp.int32)]
    if peer:
        out_shape += [jax.ShapeDtypeStruct(x.shape, x.dtype) for x in factors]
    elif not held:
        scratch_shapes += [pltpu.VMEM(x.shape, x.dtype) for x in factors]
    if peer is None or peer:
        scratch_shapes += [pltpu.VMEM(shape, acts.dtype) for shape in bufs]
    if peer is not None:
        out_shape += [jax.ShapeDtypeStruct(shape, acts.dtype) for shape in bufs]
    scratch_shapes += [
        pltpu.SemaphoreType.DMA((2, blocks)),
        pltpu.SemaphoreType.DMA((3 + 2 * count,)),
    ]
    return pl.pallas_call(
        functools.partial(project_kernel, peer, count, slot, bool(held)),
        out_shape=out_shape,
        in_specs=in_specs,
        out_specs=[VMEM] * len(out_shape),
        scratch_shapes=scratch_shapes,
        input_output_aliases={5: 1, 6: 2} if held else {},
        compiler_params=pltpu.CompilerParams(
            vmem_limit_bytes=(6 << 20) if held else 2 * (rows + width) * depth + (4 << 20)
        ),
        cost_estimate=pl.CostEstimate(
            flops=width * rows * depth, bytes_accessed=2 * rows * depth, transcendentals=0
        ),
        name="project",
    )(*operands)


def hi_lo(x):
    hi = x.astype(jnp.bfloat16)
    return hi, (x - hi.astype(jnp.float32)).astype(jnp.bfloat16)


def unit_kernel(count, rank, near, rest, *refs):
    parts, out, square, cols = refs[:-3], refs[-3], refs[-2], refs[-1]
    here = lax.axis_index("dp")
    split, per = cols.shape[1], square.shape[1] // cols.shape[1]
    for e in range(count):
        total = parts[0][e]
        for part in parts[1:]:
            total = total + part[e]
        grads = jnp.concatenate(hi_lo(total[:, :rank]), axis=1)
        acts = jnp.concatenate(hi_lo(total[:, rank:]), axis=1)
        both = lax.dot_general(grads, acts, TN, preferred_element_type=jnp.float32)
        width = total.shape[1] - rank
        kron = (both[:rank, :width] + both[rank:, width:]) + (
            both[:rank, width:] + both[rank:, :width]
        )
        norm = jnp.sqrt(jnp.sum(kron * kron, keepdims=True) + 1e-06)
        square[e] = kron / norm
        cols[e] = jnp.concatenate(
            [square[e, pl.ds(c, split, stride=per), :] for c in range(per)], axis=1
        )
        for g, r in enumerate(rest):
            for k, m in enumerate(near):
                out[g, e, k : k + 1] = cols[e, pl.ds(here ^ (r ^ m), 1), :]


def units(parts, count, slot, rank, split, near, rest):
    width = parts[0].shape[-1]
    piece = rank * (width - rank) // split
    parts = [part.reshape(count, slot, width) for part in parts]
    return pl.pallas_call(
        functools.partial(unit_kernel, count, rank, near, rest),
        out_shape=jax.ShapeDtypeStruct((len(rest), count, len(near), piece), jnp.float32),
        in_specs=[VMEM] * len(parts),
        out_specs=VMEM,
        scratch_shapes=[
            pltpu.VMEM((count, rank, width - rank), jnp.float32),
            pltpu.VMEM((count, split, piece), jnp.float32),
        ],
        compiler_params=pltpu.CompilerParams(vmem_limit_bytes=8 << 20),
        name="units",
    )(*parts)


def score_kernel(sources, halves, *refs):
    rows_of, blocks, outs = refs[:sources], refs[sources:-sources], refs[-sources:]
    count = rows_of[0].shape[0]
    rows_all = count * sources
    total = jnp.zeros((rows_all, outs[0].shape[1]), jnp.float32)
    for m, block in enumerate(blocks):
        rows = jnp.concatenate(
            [ref[e, m : m + 1, :] for ref in rows_of for e in range(count)], axis=0
        )
        rows_hi, rows_lo = hi_lo(rows)
        block_hi, block_lo = hi_lo(block[...])
        both = lax.dot_general(
            jnp.concatenate([rows_hi, rows_lo], axis=0), block_hi, NT,
            preferred_element_type=jnp.float32,
        )
        cross = lax.dot_general(rows_hi, block_lo, NT, preferred_element_type=jnp.float32)
        total = total + (both[:rows_all] + (both[rows_all:] + cross))
    for g, out in enumerate(outs):
        mine = total[g * count : (g + 1) * count]
        if halves:
            turned = jnp.concatenate([mine[count // 2 :], mine[: count // 2]], axis=0)
            mine = jnp.where(lax.axis_index("tensor") == 1, turned, mine)
        out[...] = mine


def partial_scores(rows_of, blocks, halves):
    sources = len(rows_of)
    shape = jax.ShapeDtypeStruct((rows_of[0].shape[0], blocks[0].shape[0]), jnp.float32)
    return pl.pallas_call(
        functools.partial(score_kernel, sources, halves),
        out_shape=[shape] * sources,
        in_specs=[VMEM] * (sources + len(blocks)),
        out_specs=[VMEM] * sources,
        compiler_params=pltpu.CompilerParams(vmem_limit_bytes=16 << 20),
        name="scores",
    )(*rows_of, *blocks)


def span(bits):
    masks = [0]
    for bit in bits:
        masks = masks + [m ^ bit for m in masks]
    return masks


def on_device(acts, out_grads, proj_in, proj_out, lengths, queries, query_ids):
    rank_out = proj_out.shape[0]
    ex_count = lengths.shape[0]
    slot = acts.shape[0] // ex_count
    split = lax.axis_size("dp")
    bits = [1 << i for i in range(split.bit_length() - 1)]
    near = span(bits[:NEAR_BITS])
    rest = span(bits[NEAR_BITS:])
    halves = lax.axis_size("tensor") == 2 and ex_count % 2 == 0
    args = (lengths, acts, out_grads, proj_in, proj_out)
    blocks = {0: queries}
    for m in near:
        if m == 1 or m % 2 == 0 and m > 0:
            blocks[m] = swap(queries, m)
    if halves:
        count = ex_count // 2
        theirs, *held = project(True, count, slot, *args)
        arrived = lax.ppermute(theirs, "tensor", [(0, 1), (1, 0)])
        parts = [project(False, count, slot, *args[:3], held=held)[0], arrived]
    else:
        count = ex_count
        parts = [lax.psum(project(None, count, slot, *args)[0], "tensor")]
    early = [m for m in reversed(bits[:NEAR_BITS])]
    held, parts[0] = lax.optimization_barrier(([blocks[m] for m in early], parts[0]))
    blocks.update(zip(early, held))
    own = units(parts, count, slot, rank_out, split, near, rest)
    if halves:
        own = jnp.concatenate([own, lax.ppermute(own, "tensor", [(0, 1), (1, 0)])], axis=1)
        own, blocks = lax.optimization_barrier((own, blocks))
    rows_of = [own[g] if r == 0 else swap(own[g], r) for g, r in enumerate(rest)]
    for m in near:
        if m > 1 and m % 2 == 1:
            blocks[m] = swap(blocks[m ^ 1], 1)
    sums = partial_scores(rows_of, [blocks[m] for m in near], halves)
    scores = sums[0]
    for r, got in zip(rest[1:], sums[1:]):
        scores = scores + swap(got, r)
    example_ids = lax.axis_index("dp") * ex_count + lax.broadcasted_iota(
        jnp.int32, (ex_count, 1), 0
    )
    same = example_ids == query_ids[None, :]
    return jnp.where(same, jnp.zeros_like(scores), scores)


def solution(mesh):
    in_specs = (
        P("dp", "tensor"),
        P("dp", "tensor"),
        P(None, "tensor"),
        P(None, "tensor"),
        P("dp"),
        P("tensor", "dp"),
        P("tensor"),
    )
    out_specs = P("dp", "tensor")
    return jax.shard_map(
        on_device, mesh=mesh, in_specs=in_specs, out_specs=out_specs, check_vma=False
    )
```

```python
import functools

import jax
import jax.numpy as jnp
from jax import lax
from jax.experimental import pallas as pl
from jax.experimental.pallas import tpu as pltpu
from jax.sharding import PartitionSpec as P

BLOCK = 64
WINDOW = 5
NEAR_BITS = 3
NT = (((1,), (1,)), ((), ()))
TN = (((0,), (0,)), ((), ()))
HBM = pl.BlockSpec(memory_space=pltpu.HBM)
VMEM = pl.BlockSpec(memory_space=pltpu.VMEM)


def xor_pairs(size, mask):
    return [(i, i ^ mask) for i in range(size)]


def swap(x, mask):
    return lax.ppermute(x, "dp", xor_pairs(lax.axis_size("dp"), mask))


def project_kernel(peer, count, slot, held, lengths, acts, grads, *refs):
    if held:
        in_buf, out_buf, _, _, out, act_buf, grad_buf, sems, small = refs
        used = lengths
    elif peer:
        proj_in, proj_out, out, in_buf, out_buf, next_act, next_grad = refs[:7]
        used, act_buf, grad_buf, sems, small = refs[7:]
    else:
        proj_in, proj_out, out, used, in_buf, out_buf, act_buf, grad_buf, sems, small = refs
    per = slot // BLOCK
    blocks = count * per
    first = other = 0
    if peer is not None:
        mine = lax.axis_index("tensor")
        first = (1 - mine if peer else mine) * count
        other = count - first
    rank = out_buf.shape[0]

    def copies(j):
        row = pl.multiple_of(first * slot + j * BLOCK, BLOCK)
        return (
            pltpu.make_async_copy(grads.at[pl.ds(row, BLOCK)], grad_buf.at[j], sems.at[0, j]),
            pltpu.make_async_copy(acts.at[pl.ds(row, BLOCK)], act_buf.at[j], sems.at[1, j]),
        )

    def left(j):
        return used[first + j // per] - (j % per) * BLOCK

    if not held:
        get_used = pltpu.make_async_copy(lengths, used, small.at[0])
        get_used.start()
    ahead = []
    if not held:
        get_out = pltpu.make_async_copy(proj_out, out_buf, small.at[1])
        get_in = pltpu.make_async_copy(proj_in, in_buf, small.at[2])
        get_out.start()
        get_in.start()
        for copy in copies(0):
            copy.start()
    if peer:
        for e in range(count):
            row = pl.multiple_of((other + e) * slot, BLOCK)
            for data, buf in ((grads, next_grad), (acts, next_act)):
                ahead.append(
                    pltpu.make_async_copy(
                        data.at[pl.ds(row, BLOCK)], buf.at[e * per], small.at[3 + len(ahead)]
                    )
                )
    if not held:
        get_used.wait()

    def place(i):
        if not held:
            return i
        rest = i - count
        later = rest // (per - 1) * per + rest % (per - 1) + 1
        return jnp.where(i < count, i * per, later)

    def fetch(i):
        j = place(jnp.minimum(i, blocks - 1))

        @pl.when((i < blocks) & (left(j) > 0))
        def _():
            for copy in copies(j):
                copy.start()

    @pl.loop(count if held else 1, WINDOW if held else blocks)
    def _(i):
        fetch(i)

    if not held:
        get_out.wait()
        get_in.wait()

    @pl.loop(0, blocks)
    def _(i):
        j = place(i)
        rows = left(j)
        if held:
            fetch(i + WINDOW)
        if peer:

            @pl.when(i == 2)
            def _():
                for copy in ahead:
                    copy.start()

        @pl.when(rows > 0)
        def _():
            if held:

                @pl.when(i >= count)
                def _():
                    for copy in copies(j):
                        copy.wait()
            else:
                for copy in copies(j):
                    copy.wait()
            part_grads = lax.dot_general(
                grad_buf[j], out_buf[...], NT, preferred_element_type=jnp.float32
            )
            part_acts = lax.dot_general(
                act_buf[j], in_buf[...], NT, preferred_element_type=jnp.float32
            )
            joined = jnp.concatenate([part_grads, part_acts], axis=1)
            row = lax.broadcasted_iota(jnp.int32, joined.shape, 0)
            out[j] = jnp.where(row < rows, joined, 0.0)

        @pl.when(rows <= 0)
        def _():
            out[j] = jnp.zeros((BLOCK, 2 * rank), jnp.float32)

    for copy in ahead:
        copy.wait()


def project(peer, count, slot, *args, held=()):
    lengths, acts, grads = args[:3]
    blocks = count * slot // BLOCK
    factors = held[:2] if held else args[3:]
    width = factors[0].shape[0] + factors[1].shape[0]
    rows = blocks * BLOCK
    depth = acts.shape[1] + grads.shape[1]
    outside = args[:3] if held else args
    operands = [pltpu.with_memory_space_constraint(x, pltpu.HBM) for x in outside] + [*held]
    in_specs = [HBM] * len(outside) + [VMEM] * len(held)
    if held:
        operands[0], in_specs[0] = lengths, pl.BlockSpec(memory_space=pltpu.SMEM)
    bufs = [(blocks, BLOCK, acts.shape[1]), (blocks, BLOCK, grads.shape[1])]
    out_shape = [jax.ShapeDtypeStruct((blocks, BLOCK, width), jnp.float32)]
    scratch_shapes = [] if held else [pltpu.SMEM(lengths.shape, jnp.int32)]
    if peer:
        out_shape += [jax.ShapeDtypeStruct(x.shape, x.dtype) for x in factors]
    elif not held:
        scratch_shapes += [pltpu.VMEM(x.shape, x.dtype) for x in factors]
    if peer is None or peer:
        scratch_shapes += [pltpu.VMEM(shape, acts.dtype) for shape in bufs]
    if peer is not None:
        out_shape += [jax.ShapeDtypeStruct(shape, acts.dtype) for shape in bufs]
    scratch_shapes += [
        pltpu.SemaphoreType.DMA((2, blocks)),
        pltpu.SemaphoreType.DMA((3 + 2 * count,)),
    ]
    return pl.pallas_call(
        functools.partial(project_kernel, peer, count, slot, bool(held)),
        out_shape=out_shape,
        in_specs=in_specs,
        out_specs=[VMEM] * len(out_shape),
        scratch_shapes=scratch_shapes,
        input_output_aliases={5: 1, 6: 2} if held else {},
        compiler_params=pltpu.CompilerParams(
            vmem_limit_bytes=(6 << 20) if held else 2 * (rows + width) * depth + (4 << 20)
        ),
        cost_estimate=pl.CostEstimate(
            flops=width * rows * depth, bytes_accessed=2 * rows * depth, transcendentals=0
        ),
        name="project",
    )(*operands)


def hi_lo(x):
    hi = x.astype(jnp.bfloat16)
    return hi, (x - hi.astype(jnp.float32)).astype(jnp.bfloat16)


def unit_kernel(count, rank, near, rest, *refs):
    parts, out, square, cols = refs[:-3], refs[-3], refs[-2], refs[-1]
    here = lax.axis_index("dp")
    split, per = cols.shape[1], square.shape[1] // cols.shape[1]
    for e in range(count):
        total = parts[0][e]
        for part in parts[1:]:
            total = total + part[e]
        grads = jnp.concatenate(hi_lo(total[:, :rank]), axis=1)
        acts = jnp.concatenate(hi_lo(total[:, rank:]), axis=1)
        both = lax.dot_general(grads, acts, TN, preferred_element_type=jnp.float32)
        width = total.shape[1] - rank
        kron = (both[:rank, :width] + both[rank:, width:]) + (
            both[:rank, width:] + both[rank:, :width]
        )
        norm = jnp.sqrt(jnp.sum(kron * kron, keepdims=True) + 1e-06)
        square[e] = kron / norm
        cols[e] = jnp.concatenate(
            [square[e, pl.ds(c, split, stride=per), :] for c in range(per)], axis=1
        )
        for g, r in enumerate(rest):
            for k, m in enumerate(near):
                out[g, e, k : k + 1] = cols[e, pl.ds(here ^ (r ^ m), 1), :]


def units(parts, count, slot, rank, split, near, rest):
    width = parts[0].shape[-1]
    piece = rank * (width - rank) // split
    parts = [part.reshape(count, slot, width) for part in parts]
    return pl.pallas_call(
        functools.partial(unit_kernel, count, rank, near, rest),
        out_shape=jax.ShapeDtypeStruct((len(rest), count, len(near), piece), jnp.float32),
        in_specs=[VMEM] * len(parts),
        out_specs=VMEM,
        scratch_shapes=[
            pltpu.VMEM((count, rank, width - rank), jnp.float32),
            pltpu.VMEM((count, split, piece), jnp.float32),
        ],
        compiler_params=pltpu.CompilerParams(vmem_limit_bytes=8 << 20),
        name="units",
    )(*parts)


def score_kernel(sources, halves, *refs):
    rows_of, blocks, outs = refs[:sources], refs[sources:-sources], refs[-sources:]
    count = rows_of[0].shape[0]
    rows_all = count * sources
    total = jnp.zeros((rows_all, outs[0].shape[1]), jnp.float32)
    for m, block in enumerate(blocks):
        rows = jnp.concatenate(
            [ref[e, m : m + 1, :] for ref in rows_of for e in range(count)], axis=0
        )
        rows_hi, rows_lo = hi_lo(rows)
        block_hi, block_lo = hi_lo(block[...])
        both = lax.dot_general(
            jnp.concatenate([rows_hi, rows_lo], axis=0), block_hi, NT,
            preferred_element_type=jnp.float32,
        )
        cross = lax.dot_general(rows_hi, block_lo, NT, preferred_element_type=jnp.float32)
        total = total + (both[:rows_all] + (both[rows_all:] + cross))
    for g, out in enumerate(outs):
        mine = total[g * count : (g + 1) * count]
        if halves:
            turned = jnp.concatenate([mine[count // 2 :], mine[: count // 2]], axis=0)
            mine = jnp.where(lax.axis_index("tensor") == 1, turned, mine)
        out[...] = mine


def partial_scores(rows_of, blocks, halves):
    sources = len(rows_of)
    shape = jax.ShapeDtypeStruct((rows_of[0].shape[0], blocks[0].shape[0]), jnp.float32)
    return pl.pallas_call(
        functools.partial(score_kernel, sources, halves),
        out_shape=[shape] * sources,
        in_specs=[VMEM] * (sources + len(blocks)),
        out_specs=[VMEM] * sources,
        compiler_params=pltpu.CompilerParams(vmem_limit_bytes=16 << 20),
        name="scores",
    )(*rows_of, *blocks)


def span(bits):
    masks = [0]
    for bit in bits:
        masks = masks + [m ^ bit for m in masks]
    return masks


def on_device(acts, out_grads, proj_in, proj_out, lengths, queries, query_ids):
    rank_out = proj_out.shape[0]
    ex_count = lengths.shape[0]
    slot = acts.shape[0] // ex_count
    split = lax.axis_size("dp")
    bits = [1 << i for i in range(split.bit_length() - 1)]
    near = span(bits[:NEAR_BITS])
    rest = span(bits[NEAR_BITS:])
    halves = lax.axis_size("tensor") == 2 and ex_count % 2 == 0
    args = (lengths, acts, out_grads, proj_in, proj_out)
    blocks = {0: queries}
    for m in near:
        if m == 1 or m % 2 == 0 and m > 0:
            blocks[m] = swap(queries, m)
    if halves:
        count = ex_count // 2
        theirs, *held = project(True, count, slot, *args)
        arrived = lax.ppermute(theirs, "tensor", [(0, 1), (1, 0)])
        parts = [project(False, count, slot, *args[:3], held=held)[0], arrived]
    else:
        count = ex_count
        parts = [lax.psum(project(None, count, slot, *args)[0], "tensor")]
    early = [m for m in reversed(bits[:NEAR_BITS])]
    held, parts[0] = lax.optimization_barrier(([blocks[m] for m in early], parts[0]))
    blocks.update(zip(early, held))
    own = units(parts, count, slot, rank_out, split, near, rest)
    own, held = lax.optimization_barrier((own, [blocks[m] for m in bits[1:NEAR_BITS]]))
    blocks.update(zip(bits[1:NEAR_BITS], held))
    last = near[-1] ^ 1
    if halves:
        own = jnp.concatenate([own, lax.ppermute(own, "tensor", [(0, 1), (1, 0)])], axis=1)
        own, blocks[last] = lax.optimization_barrier((own, blocks[last]))
    rows_of = [own[g] if r == 0 else swap(own[g], r) for g, r in enumerate(rest)]
    for m in near:
        if m > 1 and m % 2 == 1:
            blocks[m] = swap(blocks[m ^ 1], 1)
    sums = partial_scores(rows_of, [blocks[m] for m in near], halves)
    scores = sums[0]
    for r, got in zip(rest[1:], sums[1:]):
        scores = scores + swap(got, r)
    example_ids = lax.axis_index("dp") * ex_count + lax.broadcasted_iota(
        jnp.int32, (ex_count, 1), 0
    )
    same = example_ids == query_ids[None, :]
    return jnp.where(same, jnp.zeros_like(scores), scores)


def solution(mesh):
    in_specs = (
        P("dp", "tensor"),
        P("dp", "tensor"),
        P(None, "tensor"),
        P(None, "tensor"),
        P("dp"),
        P("tensor", "dp"),
        P("tensor"),
    )
    out_specs = P("dp", "tensor")
    return jax.shard_map(
        on_device, mesh=mesh, in_specs=in_specs, out_specs=out_specs, check_vma=False
    )
```

```python
import functools

import jax
import jax.numpy as jnp
from jax import lax
from jax.experimental import pallas as pl
from jax.experimental.pallas import tpu as pltpu
from jax.sharding import PartitionSpec as P

BLOCK = 64
WINDOW = 5
NEAR_BITS = 3
NT = (((1,), (1,)), ((), ()))
TN = (((0,), (0,)), ((), ()))
HBM = pl.BlockSpec(memory_space=pltpu.HBM)
VMEM = pl.BlockSpec(memory_space=pltpu.VMEM)


def xor_pairs(size, mask):
    return [(i, i ^ mask) for i in range(size)]


def swap(x, mask):
    return lax.ppermute(x, "dp", xor_pairs(lax.axis_size("dp"), mask))


def project_kernel(peer, count, slot, held, lengths, acts, grads, *refs):
    if held:
        in_buf, out_buf, _, _, out, act_buf, grad_buf, sems, small = refs
        used = lengths
    elif peer:
        proj_in, proj_out, out, in_buf, out_buf, next_act, next_grad = refs[:7]
        used, act_buf, grad_buf, sems, small = refs[7:]
    else:
        proj_in, proj_out, out, used, in_buf, out_buf, act_buf, grad_buf, sems, small = refs
    per = slot // BLOCK
    blocks = count * per
    first = other = 0
    if peer is not None:
        mine = lax.axis_index("tensor")
        first = (1 - mine if peer else mine) * count
        other = count - first
    rank = out_buf.shape[0]

    def copies(j):
        row = pl.multiple_of(first * slot + j * BLOCK, BLOCK)
        return (
            pltpu.make_async_copy(grads.at[pl.ds(row, BLOCK)], grad_buf.at[j], sems.at[0, j]),
            pltpu.make_async_copy(acts.at[pl.ds(row, BLOCK)], act_buf.at[j], sems.at[1, j]),
        )

    def left(j):
        return used[first + j // per] - (j % per) * BLOCK

    if not held:
        get_used = pltpu.make_async_copy(lengths, used, small.at[0])
        get_used.start()
    ahead = []
    if not held:
        get_out = pltpu.make_async_copy(proj_out, out_buf, small.at[1])
        get_in = pltpu.make_async_copy(proj_in, in_buf, small.at[2])
        get_out.start()
        get_in.start()
        for copy in copies(0):
            copy.start()
    if peer:
        for e in range(count):
            row = pl.multiple_of((other + e) * slot, BLOCK)
            for data, buf in ((grads, next_grad), (acts, next_act)):
                ahead.append(
                    pltpu.make_async_copy(
                        data.at[pl.ds(row, BLOCK)], buf.at[e * per], small.at[3 + len(ahead)]
                    )
                )
    if not held:
        get_used.wait()

    def place(i):
        if not held:
            return i
        rest = i - count
        later = rest // (per - 1) * per + rest % (per - 1) + 1
        return jnp.where(i < count, i * per, later)

    def fetch(i):
        j = place(jnp.minimum(i, blocks - 1))

        @pl.when((i < blocks) & (left(j) > 0))
        def _():
            for copy in copies(j):
                copy.start()

    @pl.loop(count if held else 1, WINDOW if held else blocks)
    def _(i):
        fetch(i)

    if not held:
        get_out.wait()
        get_in.wait()

    @pl.loop(0, blocks)
    def _(i):
        j = place(i)
        rows = left(j)
        if held:
            fetch(i + WINDOW)
        if peer:

            @pl.when(i == 2)
            def _():
                for copy in ahead:
                    copy.start()

        @pl.when(rows > 0)
        def _():
            if held:

                @pl.when(i >= count)
                def _():
                    for copy in copies(j):
                        copy.wait()
            else:
                for copy in copies(j):
                    copy.wait()
            part_grads = lax.dot_general(
                grad_buf[j], out_buf[...], NT, preferred_element_type=jnp.float32
            )
            part_acts = lax.dot_general(
                act_buf[j], in_buf[...], NT, preferred_element_type=jnp.float32
            )
            joined = jnp.concatenate([part_grads, part_acts], axis=1)
            row = lax.broadcasted_iota(jnp.int32, joined.shape, 0)
            out[j] = jnp.where(row < rows, joined, 0.0)

        @pl.when(rows <= 0)
        def _():
            out[j] = jnp.zeros((BLOCK, 2 * rank), jnp.float32)

    for copy in ahead:
        copy.wait()


def project(peer, count, slot, *args, held=()):
    lengths, acts, grads = args[:3]
    blocks = count * slot // BLOCK
    factors = held[:2] if held else args[3:]
    width = factors[0].shape[0] + factors[1].shape[0]
    rows = blocks * BLOCK
    depth = acts.shape[1] + grads.shape[1]
    outside = args[:3] if held else args
    operands = [pltpu.with_memory_space_constraint(x, pltpu.HBM) for x in outside] + [*held]
    in_specs = [HBM] * len(outside) + [VMEM] * len(held)
    if held:
        operands[0], in_specs[0] = lengths, pl.BlockSpec(memory_space=pltpu.SMEM)
    bufs = [(blocks, BLOCK, acts.shape[1]), (blocks, BLOCK, grads.shape[1])]
    out_shape = [jax.ShapeDtypeStruct((blocks, BLOCK, width), jnp.float32)]
    scratch_shapes = [] if held else [pltpu.SMEM(lengths.shape, jnp.int32)]
    if peer:
        out_shape += [jax.ShapeDtypeStruct(x.shape, x.dtype) for x in factors]
    elif not held:
        scratch_shapes += [pltpu.VMEM(x.shape, x.dtype) for x in factors]
    if peer is None or peer:
        scratch_shapes += [pltpu.VMEM(shape, acts.dtype) for shape in bufs]
    if peer is not None:
        out_shape += [jax.ShapeDtypeStruct(shape, acts.dtype) for shape in bufs]
    scratch_shapes += [
        pltpu.SemaphoreType.DMA((2, blocks)),
        pltpu.SemaphoreType.DMA((3 + 2 * count,)),
    ]
    return pl.pallas_call(
        functools.partial(project_kernel, peer, count, slot, bool(held)),
        out_shape=out_shape,
        in_specs=in_specs,
        out_specs=[VMEM] * len(out_shape),
        scratch_shapes=scratch_shapes,
        input_output_aliases={5: 1, 6: 2} if held else {},
        compiler_params=pltpu.CompilerParams(
            vmem_limit_bytes=(6 << 20) if held else 2 * (rows + width) * depth + (4 << 20)
        ),
        cost_estimate=pl.CostEstimate(
            flops=width * rows * depth, bytes_accessed=2 * rows * depth, transcendentals=0
        ),
        name="project",
    )(*operands)


def hi_lo(x):
    hi = x.astype(jnp.bfloat16)
    return hi, (x - hi.astype(jnp.float32)).astype(jnp.bfloat16)


def unit_kernel(count, rank, near, rest, *refs):
    parts, out, square, cols = refs[:-3], refs[-3], refs[-2], refs[-1]
    here = lax.axis_index("dp")
    split, per = cols.shape[1], square.shape[1] // cols.shape[1]
    for e in range(count):
        total = parts[0][e]
        for part in parts[1:]:
            total = total + part[e]
        grads = jnp.concatenate(hi_lo(total[:, :rank]), axis=1)
        acts = jnp.concatenate(hi_lo(total[:, rank:]), axis=1)
        both = lax.dot_general(grads, acts, TN, preferred_element_type=jnp.float32)
        width = total.shape[1] - rank
        kron = (both[:rank, :width] + both[rank:, width:]) + (
            both[:rank, width:] + both[rank:, :width]
        )
        norm = jnp.sqrt(jnp.sum(kron * kron, keepdims=True) + 1e-06)
        square[e] = kron / norm
        cols[e] = jnp.concatenate(
            [square[e, pl.ds(c, split, stride=per), :] for c in range(per)], axis=1
        )
        for g, r in enumerate(rest):
            for k, m in enumerate(near):
                out[g, e, k : k + 1] = cols[e, pl.ds(here ^ (r ^ m), 1), :]


def units(parts, count, slot, rank, split, near, rest):
    width = parts[0].shape[-1]
    piece = rank * (width - rank) // split
    parts = [part.reshape(count, slot, width) for part in parts]
    return pl.pallas_call(
        functools.partial(unit_kernel, count, rank, near, rest),
        out_shape=jax.ShapeDtypeStruct((len(rest), count, len(near), piece), jnp.float32),
        in_specs=[VMEM] * len(parts),
        out_specs=VMEM,
        scratch_shapes=[
            pltpu.VMEM((count, rank, width - rank), jnp.float32),
            pltpu.VMEM((count, split, piece), jnp.float32),
        ],
        compiler_params=pltpu.CompilerParams(vmem_limit_bytes=8 << 20),
        name="units",
    )(*parts)


def score_kernel(sources, halves, *refs):
    rows_of, blocks, outs = refs[:sources], refs[sources:-sources], refs[-sources:]
    count = rows_of[0].shape[0]
    rows_all = count * sources
    total = jnp.zeros((rows_all, outs[0].shape[1]), jnp.float32)
    for m, block in enumerate(blocks):
        rows = jnp.concatenate(
            [ref[e, m : m + 1, :] for ref in rows_of for e in range(count)], axis=0
        )
        rows_hi, rows_lo = hi_lo(rows)
        block_hi, block_lo = hi_lo(block[...])
        both = lax.dot_general(
            jnp.concatenate([rows_hi, rows_lo], axis=0), block_hi, NT,
            preferred_element_type=jnp.float32,
        )
        cross = lax.dot_general(rows_hi, block_lo, NT, preferred_element_type=jnp.float32)
        total = total + (both[:rows_all] + (both[rows_all:] + cross))
    for g, out in enumerate(outs):
        mine = total[g * count : (g + 1) * count]
        if halves:
            turned = jnp.concatenate([mine[count // 2 :], mine[: count // 2]], axis=0)
            mine = jnp.where(lax.axis_index("tensor") == 1, turned, mine)
        out[...] = mine


def partial_scores(rows_of, blocks, halves):
    sources = len(rows_of)
    shape = jax.ShapeDtypeStruct((rows_of[0].shape[0], blocks[0].shape[0]), jnp.float32)
    return pl.pallas_call(
        functools.partial(score_kernel, sources, halves),
        out_shape=[shape] * sources,
        in_specs=[VMEM] * (sources + len(blocks)),
        out_specs=[VMEM] * sources,
        compiler_params=pltpu.CompilerParams(vmem_limit_bytes=16 << 20),
        name="scores",
    )(*rows_of, *blocks)


def span(bits):
    masks = [0]
    for bit in bits:
        masks = masks + [m ^ bit for m in masks]
    return masks


def on_device(acts, out_grads, proj_in, proj_out, lengths, queries, query_ids):
    rank_out = proj_out.shape[0]
    ex_count = lengths.shape[0]
    slot = acts.shape[0] // ex_count
    split = lax.axis_size("dp")
    bits = [1 << i for i in range(split.bit_length() - 1)]
    near = span(bits[:NEAR_BITS])
    rest = span(bits[NEAR_BITS:])
    halves = lax.axis_size("tensor") == 2 and ex_count % 2 == 0
    args = (lengths, acts, out_grads, proj_in, proj_out)
    blocks = {0: queries}
    for m in near:
        if m % 2 == 0 and m > 0:
            blocks[m] = swap(queries, m)
    if halves:
        count = ex_count // 2
        theirs, *held = project(True, count, slot, *args)
        arrived = lax.ppermute(theirs, "tensor", [(0, 1), (1, 0)])
        parts = [project(False, count, slot, *args[:3], held=held)[0], arrived]
    else:
        count = ex_count
        parts = [lax.psum(project(None, count, slot, *args)[0], "tensor")]
    early = [m for m in reversed(bits[1:NEAR_BITS])]
    held, parts[0] = lax.optimization_barrier(([blocks[m] for m in early], parts[0]))
    blocks.update(zip(early, held))
    own = units(parts, count, slot, rank_out, split, near, rest)
    own, held = lax.optimization_barrier((own, [blocks[m] for m in (0, *early)]))
    blocks.update(zip((0, *early), held))
    last = near[-1] ^ 1
    if halves:
        own = jnp.concatenate([own, lax.ppermute(own, "tensor", [(0, 1), (1, 0)])], axis=1)
        own, blocks[last] = lax.optimization_barrier((own, blocks[last]))
    rows_of = [own[g] if r == 0 else swap(own[g], r) for g, r in enumerate(rest)]
    for m in near:
        if m % 2 == 1:
            blocks[m] = swap(blocks[m ^ 1], 1)
    sums = partial_scores(rows_of, [blocks[m] for m in near], halves)
    scores = sums[0]
    for r, got in zip(rest[1:], sums[1:]):
        scores = scores + swap(got, r)
    example_ids = lax.axis_index("dp") * ex_count + lax.broadcasted_iota(
        jnp.int32, (ex_count, 1), 0
    )
    same = example_ids == query_ids[None, :]
    return jnp.where(same, jnp.zeros_like(scores), scores)


def solution(mesh):
    in_specs = (
        P("dp", "tensor"),
        P("dp", "tensor"),
        P(None, "tensor"),
        P(None, "tensor"),
        P("dp"),
        P("tensor", "dp"),
        P("tensor"),
    )
    out_specs = P("dp", "tensor")
    return jax.shard_map(
        on_device, mesh=mesh, in_specs=in_specs, out_specs=out_specs, check_vma=False
    )
```
